512 devices in a mesh: dp: 64 (over z_lo, x, y), tensor: 8 (over z_hi, core).
Axes of the slice: x: 4, y: 4, z: 16 (z_hi: 4, z_lo: 4; z = z_hi * 4 + z_lo), core: 2. Of those that a mesh axis runs over, the one named last changes fastest.
Arguments:
- activations: bfloat16 [64, 256, 8192], P('dp', None, 'tensor'), may hold values from -6 to 6
- output_grads: bfloat16 [64, 256, 8192], P('dp', None, 'tensor'), may hold values from -0.375 to 0.375
- projection: bfloat16 [8192, 128], P('tensor'), may hold values from -0.0625 to 0.0625
- token_counts: int32 [64], P('dp'), may hold values from 64 to 256, as said below
- hessian_inverse: bfloat16 [4096, 4096], P('dp', 'tensor')
- queries: bfloat16 [1024, 4096], P('dp', 'tensor'), may hold values from -0.09375 to 0.09375
Outputs:
- scores: float32 [64, 1024], P('dp', 'tensor')
The draws below stay inside these ranges and needn't reach their ends.
Inputs may be any that keep to these rules, and one draw needn't show every extreme that they name: `token_counts`: in every draw some example uses all 256 positions and some uses exactly 64.
All inputs are finite; a program needn't handle non-finite values.
Results may differ from the reference program's by a relative error of at most 0.004.
Values may be sent and summed in bfloat16 or wider, within the bound.
A program may use at most 64 MiB of HBM per device.

```python
import math
import jax
import jax.numpy as jnp
from jax import lax

D = 8192
R = 64
K = 4096
LEN = 256
EXAMPLES = 64
NQ = 1024


def draw_token_counts(key, part):
    key = jax.random.fold_in(key, 11)
    first_key, second_key, third_key = jax.random.split(key, 3)
    values = jax.random.randint(first_key, (EXAMPLES,), LEN // 4, LEN + 1)
    fullest = jax.random.randint(second_key, (), 0, EXAMPLES)
    shortest = (fullest + 1 + jax.random.randint(third_key, (), 0, EXAMPLES - 1)) % EXAMPLES
    values = values.at[fullest].set(LEN)
    values = values.at[shortest].set(LEN // 4)
    return values.astype(jnp.int32)


def draw_hessian_inverse(key, part):
    key = jax.random.fold_in(key, 23)
    first_key, second_key = jax.random.split(key)
    across = jax.random.normal(first_key, (K, K), jnp.float32) * (0.5 / math.sqrt(K))
    diagonal = jnp.exp(jax.random.uniform(second_key, (K,), jnp.float32, math.log(0.5), math.log(2.0)))
    identity_mask = (jnp.arange(K)[:, None] == jnp.arange(K)[None, :]).astype(jnp.float32)
    return (across + identity_mask * diagonal[None, :]).astype(jnp.bfloat16)


def block_levels(stream_key, extent, cuts, least, top_value):
    def one(position, blocks):
        steps = jax.random.uniform(jax.random.fold_in(jax.random.fold_in(stream_key, 6), position), (blocks,), jnp.float32, least / len(cuts), top_value / len(cuts))
        return jnp.repeat(jnp.exp(steps), extent[position] // blocks).reshape((-1,) + (1,) * (len(extent) - position - 1))

    gain = one(*cuts[0])
    for cut in cuts[1:]:
        gain = gain * one(*cut)
    return gain


def bell_draw(stream_key, extent, deviation, most, cuts=(), held_as=jnp.bfloat16):
    gain = block_levels(stream_key, extent, cuts, -0.22, 0.18) if cuts else 1.0
    array = jax.random.normal(stream_key, extent, jnp.float32) * deviation * gain
    return jnp.minimum(jnp.maximum(array, -most), most).astype(held_as)


def setup_inputs(seed: int = 0) -> dict:
    splits = jax.random.split(jax.random.key(seed), 7)
    activations = bell_draw(splits[0], (EXAMPLES, LEN, D), 1.0, 6.0, ((0, 64), (2, 8)))
    output_grads = bell_draw(splits[1], (EXAMPLES, LEN, D), 0.0625, 0.375, ((0, 64), (2, 8)))
    projection = bell_draw(splits[2], (D, 2 * R), D ** -0.5, 0.0625, ((0, 8),))
    token_counts = draw_token_counts(jax.random.fold_in(splits[6], 71), 0)
    hessian_inverse = draw_hessian_inverse(jax.random.fold_in(splits[6], 71), 0)
    queries = bell_draw(splits[5], (NQ, K), K ** -0.5, 0.09375, ((0, 64), (1, 8)))
    return dict(activations=activations, output_grads=output_grads, projection=projection, token_counts=token_counts, hessian_inverse=hessian_inverse, queries=queries)


def reference(activations, output_grads, projection, token_counts, hessian_inverse, queries):
    flat_acts = activations.reshape(EXAMPLES * LEN, D)
    flat_grads = output_grads.reshape(EXAMPLES * LEN, D)
    inputs_side = jnp.dot(flat_acts, projection[:, :R], preferred_element_type=jnp.float32).reshape(EXAMPLES, LEN, R)
    output_side = jnp.dot(flat_grads, projection[:, R:], preferred_element_type=jnp.float32).reshape(EXAMPLES, LEN, R)
    inside = (jnp.arange(LEN, dtype=jnp.int32)[None, :] < token_counts[:, None]).astype(jnp.float32)
    inputs_side = inputs_side * inside[:, :, None]
    output_side = output_side * inside[:, :, None]
    outer = jnp.einsum("eta,etb->eab", output_side, inputs_side, precision=lax.Precision.HIGHEST)
    factor = outer.reshape(EXAMPLES, K).astype(jnp.bfloat16)
    preconditioned = jnp.dot(factor, hessian_inverse, preferred_element_type=jnp.float32).astype(jnp.bfloat16)
    return jnp.dot(preconditioned, queries.T, preferred_element_type=jnp.float32)
```

```python
import jax
import jax.numpy as jnp
from jax import lax
from jax.experimental import pallas as pl
from jax.experimental.pallas import tpu as pltpu
from jax.sharding import PartitionSpec as P

MESH = pl.DeviceIdType.MESH
NEAR = 16
RUNS = 4
RANK = 64
HALF = 128
PLANE = sorted(range(1, NEAR), key=lambda k: -(min(k // 4, 4 - k // 4) + min(k % 4, 4 - k % 4)))


def attribute(
    acts_hbm, grads_hbm, proj_hbm, counts_hbm, hess_hbm, query_hbm, out,
    acts, grads, proj, counts, rows, pair, wire, wires, partial, partner, factor, factors,
    hess, query, product, others, summed, blocks, gathered, part, parts,
    load_sem, send_sem, recv_sem, block_sem, known,
):
    d, s = lax.axis_index("dp"), lax.axis_index("tensor")
    run, plane = d // NEAR, lax.rem(d, NEAR)
    px, py = plane // 4, lax.rem(plane, 4)
    group, core = s // 2, lax.rem(s, 2)
    z = group * RUNS + run

    def at(run_, plane_, group_, core_):
        return (run_ * NEAR + plane_, group_ * 2 + core_)

    def ring(k):
        there = lax.rem(z + k + 16, 16)
        return at(lax.rem(there, RUNS), plane, there // RUNS, core)

    def beside(k):
        return at(run, lax.rem(px + k // 4, 4) * 4 + lax.rem(py + k % 4, 4), group, core)

    def along(k):
        return at(lax.rem(run + k, RUNS), plane, group, core)

    def across(k):
        return at(run, plane, lax.rem(group + k, RUNS), core)

    sibling = at(run, plane, group, 1 - core)

    def send(src, dst, k, device):
        pltpu.make_async_remote_copy(
            src, dst, send_sem.at[k], recv_sem.at[k], device_id=device, device_id_type=MESH
        ).start()

    def arrived(ref, k):
        pltpu.make_async_copy(ref, ref, recv_sem.at[k]).wait()

    def left(ref, k):
        pltpu.make_async_copy(ref, ref, send_sem.at[k]).wait()

    barrier = pltpu.get_barrier_semaphore()
    greeted = [beside(k) for k in PLANE] + [ring(k) for k in (4, -4, 3, -3, 2, -2, 1, -1)] + [sibling]
    for device in greeted:
        pl.semaphore_signal(barrier, inc=1, device_id=device, device_id_type=MESH)
    loads = [
        pltpu.make_async_copy(query_hbm, query.at[plane], load_sem.at[0]),
        pltpu.make_async_copy(hess_hbm, hess.at[run], load_sem.at[1]),
        pltpu.make_async_copy(proj_hbm, proj, load_sem.at[2]),
        pltpu.make_async_copy(acts_hbm, acts, load_sem.at[3]),
        pltpu.make_async_copy(grads_hbm, grads, load_sem.at[4]),
        pltpu.make_async_copy(counts_hbm, counts, load_sem.at[5]),
    ]
    for load in loads:
        load.start()

    for load in loads[2:]:
        load.wait()
    lane = lax.broadcasted_iota(jnp.int32, (2 * HALF, 2 * RANK), 1)
    position = lax.broadcasted_iota(jnp.int32, (2 * HALF, 2 * RANK), 0)
    inputs_side = jnp.dot(acts[0], proj[...], preferred_element_type=jnp.float32)
    output_side = jnp.dot(grads[0], proj[...], preferred_element_type=jnp.float32)
    projected = jnp.where(lane < RANK, inputs_side, output_side)
    projected = jnp.where(position < counts[0], projected, 0.0)
    rows[0] = projected[:HALF]
    rows[1] = projected[HALF:]
    for load in loads[:2]:
        load.wait()

    pl.semaphore_wait(barrier, len(greeted))
    for k in (4, -4):
        pl.semaphore_signal(known, inc=1, device_id=ring(k), device_id_type=MESH)
    send(rows.at[1 - core], pair, 0, sibling)
    for k in PLANE:
        send(query.at[plane], query.at[plane], 1, beside(k))
    for k in (2, 1, 3):
        send(hess.at[run], hess.at[run], 2, along(k))
    arrived(pair, 0)
    chip = rows[core] + pair[...]
    wire[...] = chip.astype(jnp.bfloat16)
    pl.semaphore_wait(known, 2)
    for k in (2, 1, 3):
        send(wire, wires.at[k - 1], 3, across(k))

    arrived(query.at[pl.ds(0, NEAR - 1)], 1)
    arrived(hess.at[pl.ds(0, RUNS - 1)], 2)
    contract = (((1,), (1,)), ((), ()))
    rows_of_hess = hess[...].reshape(RUNS * RANK, 512)

    def times(which):
        some = query[pl.ds(which * 8, 8)].reshape(HALF, 512)
        result = lax.dot_general(rows_of_hess, some, contract, preferred_element_type=jnp.float32)
        return result.reshape(RUNS, RANK, HALF)

    product[...] = times(1 - core)
    send(product, others, 4, sibling)
    own = times(core)
    arrived(others, 4)
    summed[...] = own + others[...]
    for k in range(RUNS):
        stays = jnp.logical_and(group == run, run == k)

        @pl.when(jnp.logical_not(stays))
        def _():
            pltpu.make_async_remote_copy(
                summed.at[k], blocks.at[group], block_sem.at[k], recv_sem.at[5],
                device_id=at(k, plane, run, core), device_id_type=MESH,
            ).start()

        @pl.when(stays)
        def _():
            pltpu.make_async_copy(summed.at[k], blocks.at[group], recv_sem.at[5]).start()

    arrived(wires, 3)
    whole = chip + (
        wires[0].astype(jnp.float32) + wires[1].astype(jnp.float32) + wires[2].astype(jnp.float32)
    )
    outer = lax.dot_general(
        whole, whole, (((0,), (0,)), ((), ())),
        precision=lax.Precision.HIGHEST, preferred_element_type=jnp.float32,
    )
    partial[...] = outer[RANK:]
    send(partial, partner, 6, sibling)
    arrived(partner, 6)
    rounded = (partial[...] + partner[...]).astype(jnp.bfloat16)
    to = lax.broadcasted_iota(jnp.int32, (NEAR * 8, RANK), 0)
    come = lax.broadcasted_iota(jnp.int32, (NEAR * 8, RANK), 1)
    to_run, to_plane = lax.rem(to, 8), lax.div(to, 8)
    chosen = jnp.logical_and(to_run < RUNS, come == to_run * NEAR + to_plane)
    order = jnp.where(chosen, 1.0, 0.0).astype(jnp.bfloat16)
    ordered = jnp.dot(order, rounded, preferred_element_type=jnp.float32)
    factor[...] = ordered.reshape(NEAR, 8, 2 * RANK)
    for k in PLANE:
        there = lax.rem(px + k // 4, 4) * 4 + lax.rem(py + k % 4, 4)
        send(factor.at[there], factors.at[plane], 7, beside(k))
    factors[plane] = factor[plane]

    arrived(blocks, 5)
    gathered[run] = (blocks[0] + blocks[1] + (blocks[2] + blocks[3])).astype(jnp.bfloat16)
    for k in (2, 1, 3):
        send(gathered.at[run], gathered.at[run], 8, along(k))
    arrived(factors.at[pl.ds(0, NEAR - 1)], 7)
    left_side = factors[...].reshape(NEAR * 8, 2 * RANK)[:, :RANK].astype(jnp.bfloat16)
    which = lax.rem(lax.broadcasted_iota(jnp.int32, (NEAR * 8, HALF), 0), 8)
    arrived(gathered.at[pl.ds(0, RUNS - 1)], 8)
    scores = jnp.zeros((NEAR * 8, HALF), jnp.float32)
    for k in range(RUNS):
        term = jnp.dot(left_side, gathered[k], preferred_element_type=jnp.float32)
        scores += jnp.where(which == k, term, 0.0)
    part[...] = scores.reshape(NEAR, 8, HALF)
    for k in PLANE:
        there = lax.rem(px + k // 4, 4) * 4 + lax.rem(py + k % 4, 4)
        send(part.at[there], parts.at[plane], 9, beside(k))
    parts[plane] = part[plane]

    left(pair, 0)
    left(query.at[pl.ds(0, NEAR - 1)], 1)
    left(hess.at[pl.ds(0, RUNS - 1)], 2)
    left(wires, 3)
    left(others, 4)
    left(partner, 6)
    left(factors.at[pl.ds(0, NEAR - 1)], 7)
    left(gathered.at[pl.ds(0, RUNS - 1)], 8)
    for k in range(RUNS):
        @pl.when(jnp.logical_not(jnp.logical_and(group == run, run == k)))
        def _():
            pltpu.make_async_copy(summed.at[k], summed.at[k], block_sem.at[k]).wait()
    arrived(parts.at[pl.ds(0, NEAR - 1)], 9)
    total = jnp.sum(parts[...], axis=0)
    out[...] = jnp.sum(total, axis=0, keepdims=True)
    left(parts.at[pl.ds(0, NEAR - 1)], 9)


def on_device(activations, output_grads, projection, token_counts, hessian_inverse, queries):
    anywhere = pl.BlockSpec(memory_space=pltpu.HBM)
    bf16, f32 = jnp.bfloat16, jnp.float32
    scratch = [
        pltpu.VMEM((1, 256, 1024), bf16),
        pltpu.VMEM((1, 256, 1024), bf16),
        pltpu.VMEM((1024, 128), bf16),
        pltpu.SMEM((1,), jnp.int32),
        pltpu.VMEM((2, HALF, 128), f32),
        pltpu.VMEM((HALF, 128), f32),
        pltpu.VMEM((HALF, 128), bf16),
        pltpu.VMEM((RUNS - 1, HALF, 128), bf16),
        pltpu.VMEM((RANK, 128), f32),
        pltpu.VMEM((RANK, 128), f32),
        pltpu.VMEM((NEAR, 8, 128), f32),
        pltpu.VMEM((NEAR, 8, 128), f32),
        pltpu.VMEM((RUNS, RANK, 512), bf16),
        pltpu.VMEM((NEAR, 16, 512), bf16),
        pltpu.VMEM((RUNS, RANK, HALF), f32),
        pltpu.VMEM((RUNS, RANK, HALF), f32),
        pltpu.VMEM((RUNS, RANK, HALF), f32),
        pltpu.VMEM((RUNS, RANK, HALF), f32),
        pltpu.VMEM((RUNS, RANK, HALF), bf16),
        pltpu.VMEM((NEAR, 8, HALF), f32),
        pltpu.VMEM((NEAR, 8, HALF), f32),
        pltpu.SemaphoreType.DMA((6,)),
        pltpu.SemaphoreType.DMA((10,)),
        pltpu.SemaphoreType.DMA((10,)),
        pltpu.SemaphoreType.DMA((RUNS,)),
        pltpu.SemaphoreType.REGULAR,
    ]
    return pl.pallas_call(
        attribute,
        out_shape=jax.ShapeDtypeStruct((1, HALF), f32),
        in_specs=[anywhere] * 6,
        out_specs=pl.BlockSpec(memory_space=pltpu.VMEM),
        scratch_shapes=scratch,
        compiler_params=pltpu.CompilerParams(
            collective_id=0, has_side_effects=True, vmem_limit_bytes=60 << 20
        ),
        cost_estimate=pl.CostEstimate(flops=200_000_000, bytes_accessed=1_500_000, transcendentals=0),
        name="attribute",
    )(activations, output_grads, projection, token_counts, hessian_inverse, queries)


def solution(mesh):
    placed = (
        P("dp", None, "tensor"),
        P("dp", None, "tensor"),
        P("tensor", None),
        P("dp"),
        P("dp", "tensor"),
        P("dp", "tensor"),
    )
    return jax.shard_map(
        on_device, mesh=mesh, in_specs=placed, out_specs=P("dp", "tensor"), check_vma=False
    )
```

```python
import jax
import jax.numpy as jnp
from jax import lax
from jax.experimental import pallas as pl
from jax.experimental.pallas import tpu as pltpu
from jax.sharding import PartitionSpec as P

MESH = pl.DeviceIdType.MESH
NEAR = 16
RUNS = 4
RANK = 64
HALF = 128
PLANE = sorted(range(1, NEAR), key=lambda k: -(min(k // 4, 4 - k // 4) + min(k % 4, 4 - k % 4)))


def encode(values):
    most = jnp.maximum(jnp.max(jnp.abs(values), axis=0, keepdims=True), 1e-30)
    codes = jnp.round(values * (32000.0 / most)).astype(jnp.int32).astype(jnp.int16)
    return codes, jnp.broadcast_to(most * (1.0 / 32000.0), (8, 128))


def decode(codes, scales):
    return codes.astype(jnp.int32).astype(jnp.float32) * scales[:1]


def attribute(
    acts_hbm, grads_hbm, proj_hbm, counts_hbm, hess_hbm, query_hbm, out,
    acts, grads, proj, counts, rows, pair, codes, codes_in, scales, scales_in, partial, partner, factor, factors,
    hess, query, product, others, summed, blocks, gathered, part, parts,
    load_sem, send_sem, recv_sem, block_sem, known,
):
    d, s = lax.axis_index("dp"), lax.axis_index("tensor")
    run, plane = d // NEAR, lax.rem(d, NEAR)
    px, py = plane // 4, lax.rem(plane, 4)
    group, core = s // 2, lax.rem(s, 2)
    z = group * RUNS + run

    def at(run_, plane_, group_, core_):
        return (run_ * NEAR + plane_, group_ * 2 + core_)

    def ring(k):
        there = lax.rem(z + k + 16, 16)
        return at(lax.rem(there, RUNS), plane, there // RUNS, core)

    def beside(k):
        return at(run, lax.rem(px + k // 4, 4) * 4 + lax.rem(py + k % 4, 4), group, core)

    def along(k):
        return at(lax.rem(run + k, RUNS), plane, group, core)

    def across(k):
        return at(run, plane, lax.rem(group + k, RUNS), core)

    sibling = at(run, plane, group, 1 - core)

    def send(src, dst, k, device):
        pltpu.make_async_remote_copy(
            src, dst, send_sem.at[k], recv_sem.at[k], device_id=device, device_id_type=MESH
        ).start()

    def arrived(ref, k):
        pltpu.make_async_copy(ref, ref, recv_sem.at[k]).wait()

    def left(ref, k):
        pltpu.make_async_copy(ref, ref, send_sem.at[k]).wait()

    barrier = pltpu.get_barrier_semaphore()
    greeted = [beside(k) for k in PLANE] + [ring(k) for k in (4, -4, 3, -3, 2, -2, 1, -1)] + [sibling]
    for device in greeted:
        pl.semaphore_signal(barrier, inc=1, device_id=device, device_id_type=MESH)
    loads = [
        pltpu.make_async_copy(query_hbm, query.at[plane], load_sem.at[0]),
        pltpu.make_async_copy(hess_hbm, hess.at[run], load_sem.at[1]),
        pltpu.make_async_copy(proj_hbm, proj, load_sem.at[2]),
        pltpu.make_async_copy(acts_hbm, acts, load_sem.at[3]),
        pltpu.make_async_copy(grads_hbm, grads, load_sem.at[4]),
        pltpu.make_async_copy(counts_hbm, counts, load_sem.at[5]),
    ]
    for load in loads:
        load.start()

    for load in loads[2:]:
        load.wait()
    lane = lax.broadcasted_iota(jnp.int32, (2 * HALF, 2 * RANK), 1)
    position = lax.broadcasted_iota(jnp.int32, (2 * HALF, 2 * RANK), 0)
    inputs_side = jnp.dot(acts[0], proj[...], preferred_element_type=jnp.float32)
    output_side = jnp.dot(grads[0], proj[...], preferred_element_type=jnp.float32)
    projected = jnp.where(lane < RANK, inputs_side, output_side)
    projected = jnp.where(position < counts[0], projected, 0.0)
    rows[0] = projected[:HALF]
    rows[1] = projected[HALF:]
    for load in loads[:2]:
        load.wait()

    pl.semaphore_wait(barrier, len(greeted))
    for k in (4, -4):
        pl.semaphore_signal(known, inc=1, device_id=ring(k), device_id_type=MESH)
    send(rows.at[1 - core], pair, 0, sibling)
    for k in PLANE:
        send(query.at[plane], query.at[plane], 1, beside(k))
    for k in (2, 1, 3):
        send(hess.at[run], hess.at[run], 2, along(k))
    arrived(pair, 0)
    chip = rows[core] + pair[...]
    halves = [chip[: HALF // 2], chip[HALF // 2 :]]
    for step in range(2):
        for half in range(2):
            slot = 2 * step + half
            codes[slot], scales[slot] = encode(halves[half])
            partner_group = lax.rem(group + 1 + 2 * lax.rem(group + slot // 2 + half, 2), RUNS)
            device = at(run, plane, partner_group, core)
            send(codes.at[slot], codes_in.at[slot], 10 + slot, device)
            send(scales.at[slot], scales_in.at[slot], 14 + slot, device)
        if step == 0:
            for half in range(2):
                arrived(codes.at[half], 10 + half)
                arrived(scales.at[half], 14 + half)
                halves[half] = halves[half] + decode(codes_in[half], scales_in[half])

    arrived(query.at[pl.ds(0, NEAR - 1)], 1)
    arrived(hess.at[pl.ds(0, RUNS - 1)], 2)
    contract = (((1,), (1,)), ((), ()))
    rows_of_hess = hess[...].reshape(RUNS * RANK, 512)

    def times(which):
        some = query[pl.ds(which * 8, 8)].reshape(HALF, 512)
        result = lax.dot_general(rows_of_hess, some, contract, preferred_element_type=jnp.float32)
        return result.reshape(RUNS, RANK, HALF)

    product[...] = times(1 - core)
    send(product, others, 4, sibling)
    own = times(core)
    arrived(others, 4)
    summed[...] = (own + others[...]).astype(jnp.bfloat16)
    pl.semaphore_wait(known, 2)
    for k in range(RUNS):
        stays = jnp.logical_and(group == run, run == k)

        @pl.when(jnp.logical_not(stays))
        def _():
            pltpu.make_async_remote_copy(
                summed.at[k], blocks.at[group], block_sem.at[k], recv_sem.at[5],
                device_id=at(k, plane, run, core), device_id_type=MESH,
            ).start()

        @pl.when(stays)
        def _():
            pltpu.make_async_copy(summed.at[k], blocks.at[group], recv_sem.at[5]).start()

    for half in range(2):
        arrived(codes.at[2 + half], 12 + half)
        arrived(scales.at[2 + half], 16 + half)
        halves[half] = halves[half] + decode(codes_in[2 + half], scales_in[2 + half])
    whole = jnp.concatenate(halves, axis=0)
    outer = lax.dot_general(
        whole, whole, (((0,), (0,)), ((), ())),
        precision=lax.Precision.HIGHEST, preferred_element_type=jnp.float32,
    )
    partial[...] = outer[RANK:]
    send(partial, partner, 6, sibling)
    arrived(partner, 6)
    rounded = (partial[...] + partner[...]).astype(jnp.bfloat16)
    to = lax.broadcasted_iota(jnp.int32, (NEAR * 8, RANK), 0)
    come = lax.broadcasted_iota(jnp.int32, (NEAR * 8, RANK), 1)
    to_run, to_plane = lax.rem(to, 8), lax.div(to, 8)
    chosen = jnp.logical_and(to_run < RUNS, come == to_run * NEAR + to_plane)
    order = jnp.where(chosen, 1.0, 0.0).astype(jnp.bfloat16)
    ordered = jnp.dot(order, rounded, preferred_element_type=jnp.float32)
    factor[...] = ordered.reshape(NEAR, 8, 2 * RANK)
    for k in PLANE:
        there = lax.rem(px + k // 4, 4) * 4 + lax.rem(py + k % 4, 4)
        send(factor.at[there], factors.at[plane], 7, beside(k))
    factors[plane] = factor[plane]

    arrived(blocks, 5)
    b = blocks[...].astype(jnp.float32)
    gathered[run] = (b[0] + b[1] + (b[2] + b[3])).astype(jnp.bfloat16)
    for k in (2, 1, 3):
        send(gathered.at[run], gathered.at[run], 8, along(k))
    arrived(factors.at[pl.ds(0, NEAR - 1)], 7)
    left_side = factors[...].reshape(NEAR * 8, 2 * RANK)[:, :RANK].astype(jnp.bfloat16)
    which = lax.rem(lax.broadcasted_iota(jnp.int32, (NEAR * 8, HALF), 0), 8)
    arrived(gathered.at[pl.ds(0, RUNS - 1)], 8)
    scores = jnp.zeros((NEAR * 8, HALF), jnp.float32)
    for k in range(RUNS):
        term = jnp.dot(left_side, gathered[k], preferred_element_type=jnp.float32)
        scores += jnp.where(which == k, term, 0.0)
    part[...] = scores.reshape(NEAR, 8, HALF)
    for k in PLANE:
        there = lax.rem(px + k // 4, 4) * 4 + lax.rem(py + k % 4, 4)
        send(part.at[there], parts.at[plane], 9, beside(k))
    parts[plane] = part[plane]

    left(pair, 0)
    left(query.at[pl.ds(0, NEAR - 1)], 1)
    left(hess.at[pl.ds(0, RUNS - 1)], 2)
    for slot in range(4):
        left(codes.at[slot], 10 + slot)
        left(scales.at[slot], 14 + slot)
    left(others, 4)
    left(partner, 6)
    left(factors.at[pl.ds(0, NEAR - 1)], 7)
    left(gathered.at[pl.ds(0, RUNS - 1)], 8)
    for k in range(RUNS):
        @pl.when(jnp.logical_not(jnp.logical_and(group == run, run == k)))
        def _():
            pltpu.make_async_copy(summed.at[k], summed.at[k], block_sem.at[k]).wait()
    arrived(parts.at[pl.ds(0, NEAR - 1)], 9)
    total = jnp.sum(parts[...], axis=0)
    out[...] = jnp.sum(total, axis=0, keepdims=True)
    left(parts.at[pl.ds(0, NEAR - 1)], 9)


def on_device(activations, output_grads, projection, token_counts, hessian_inverse, queries):
    anywhere = pl.BlockSpec(memory_space=pltpu.HBM)
    bf16, f32 = jnp.bfloat16, jnp.float32
    scratch = [
        pltpu.VMEM((1, 256, 1024), bf16),
        pltpu.VMEM((1, 256, 1024), bf16),
        pltpu.VMEM((1024, 128), bf16),
        pltpu.SMEM((1,), jnp.int32),
        pltpu.VMEM((2, HALF, 128), f32),
        pltpu.VMEM((HALF, 128), f32),
        pltpu.VMEM((4, HALF // 2, 128), jnp.int16),
        pltpu.VMEM((4, HALF // 2, 128), jnp.int16),
        pltpu.VMEM((4, 8, 128), f32),
        pltpu.VMEM((4, 8, 128), f32),
        pltpu.VMEM((RANK, 128), f32),
        pltpu.VMEM((RANK, 128), f32),
        pltpu.VMEM((NEAR, 8, 128), f32),
        pltpu.VMEM((NEAR, 8, 128), f32),
        pltpu.VMEM((RUNS, RANK, 512), bf16),
        pltpu.VMEM((NEAR, 16, 512), bf16),
        pltpu.VMEM((RUNS, RANK, HALF), f32),
        pltpu.VMEM((RUNS, RANK, HALF), f32),
        pltpu.VMEM((RUNS, RANK, HALF), bf16),
        pltpu.VMEM((RUNS, RANK, HALF), bf16),
        pltpu.VMEM((RUNS, RANK, HALF), bf16),
        pltpu.VMEM((NEAR, 8, HALF), f32),
        pltpu.VMEM((NEAR, 8, HALF), f32),
        pltpu.SemaphoreType.DMA((6,)),
        pltpu.SemaphoreType.DMA((18,)),
        pltpu.SemaphoreType.DMA((18,)),
        pltpu.SemaphoreType.DMA((RUNS,)),
        pltpu.SemaphoreType.REGULAR,
    ]
    return pl.pallas_call(
        attribute,
        out_shape=jax.ShapeDtypeStruct((1, HALF), f32),
        in_specs=[anywhere] * 6,
        out_specs=pl.BlockSpec(memory_space=pltpu.VMEM),
        scratch_shapes=scratch,
        compiler_params=pltpu.CompilerParams(
            collective_id=0, has_side_effects=True, vmem_limit_bytes=60 << 20
        ),
        cost_estimate=pl.CostEstimate(flops=200_000_000, bytes_accessed=1_500_000, transcendentals=0),
        name="attribute",
    )(activations, output_grads, projection, token_counts, hessian_inverse, queries)


def solution(mesh):
    placed = (
        P("dp", None, "tensor"),
        P("dp", None, "tensor"),
        P("tensor", None),
        P("dp"),
        P("dp", "tensor"),
        P("dp", "tensor"),
    )
    return jax.shard_map(
        on_device, mesh=mesh, in_specs=placed, out_specs=P("dp", "tensor"), check_vma=False
    )
```

```python
import jax
import jax.numpy as jnp
from jax import lax
from jax.experimental import pallas as pl
from jax.experimental.pallas import tpu as pltpu
from jax.sharding import PartitionSpec as P

MESH = pl.DeviceIdType.MESH
NEAR = 16
RUNS = 4
RANK = 64
HALF = 128
PLANE = sorted(range(1, NEAR), key=lambda k: -(min(k // 4, 4 - k // 4) + min(k % 4, 4 - k % 4)))


def encode(values):
    most = jnp.maximum(jnp.max(jnp.abs(values), axis=0, keepdims=True), 1e-30)
    codes = jnp.round(values * (32000.0 / most)).astype(jnp.int32).astype(jnp.int16)
    return codes, jnp.broadcast_to(most * (1.0 / 32000.0), (8, 128))


def decode(codes, scales):
    return codes.astype(jnp.int32).astype(jnp.float32) * scales[:1]


def attribute(
    acts_hbm, grads_hbm, proj_hbm, counts_hbm, hess_hbm, query_hbm, out,
    acts, grads, proj, counts, rows, pair, codes, codes_in, scales, scales_in, partial, partner, factor, factors,
    hess, query, product, others, summed, blocks, gathered, part, parts,
    load_sem, send_sem, recv_sem,
):
    d, s = lax.axis_index("dp"), lax.axis_index("tensor")
    run, plane = d // NEAR, lax.rem(d, NEAR)
    px, py = plane // 4, lax.rem(plane, 4)
    group, core = s // 2, lax.rem(s, 2)

    def at(run_, plane_, group_, core_):
        return (run_ * NEAR + plane_, group_ * 2 + core_)

    def beside(k):
        return at(run, lax.rem(px + k // 4, 4) * 4 + lax.rem(py + k % 4, 4), group, core)

    def along(k):
        return at(lax.rem(run + k, RUNS), plane, group, core)

    def across(k):
        return at(run, plane, lax.rem(group + k, RUNS), core)

    sibling = at(run, plane, group, 1 - core)

    def send(src, dst, k, device):
        pltpu.make_async_remote_copy(
            src, dst, send_sem.at[k], recv_sem.at[k], device_id=device, device_id_type=MESH
        ).start()

    def arrived(ref, k):
        pltpu.make_async_copy(ref, ref, recv_sem.at[k]).wait()

    def left(ref, k):
        pltpu.make_async_copy(ref, ref, send_sem.at[k]).wait()

    barrier = pltpu.get_barrier_semaphore()
    greeted = [across(1), across(3)] + [along(k) for k in (2, 1, 3)] + [beside(k) for k in (8, 2, 4, 12, 1, 3)] + [sibling]
    for device in greeted:
        pl.semaphore_signal(barrier, inc=1, device_id=device, device_id_type=MESH)
    loads = [
        pltpu.make_async_copy(query_hbm, query.at[px, run], load_sem.at[0]),
        pltpu.make_async_copy(hess_hbm, hess.at[py], load_sem.at[1]),
        pltpu.make_async_copy(proj_hbm, proj, load_sem.at[2]),
        pltpu.make_async_copy(acts_hbm, acts, load_sem.at[3]),
        pltpu.make_async_copy(grads_hbm, grads, load_sem.at[4]),
        pltpu.make_async_copy(counts_hbm, counts, load_sem.at[5]),
    ]
    for load in loads:
        load.start()

    for load in loads[2:]:
        load.wait()
    lane = lax.broadcasted_iota(jnp.int32, (2 * HALF, 2 * RANK), 1)
    position = lax.broadcasted_iota(jnp.int32, (2 * HALF, 2 * RANK), 0)
    inputs_side = jnp.dot(acts[0], proj[...], preferred_element_type=jnp.float32)
    output_side = jnp.dot(grads[0], proj[...], preferred_element_type=jnp.float32)
    projected = jnp.where(lane < RANK, inputs_side, output_side)
    projected = jnp.where(position < counts[0], projected, 0.0)
    rows[0] = projected[:HALF]
    rows[1] = projected[HALF:]
    for load in loads[:2]:
        load.wait()

    pl.semaphore_wait(barrier, len(greeted))
    send(rows.at[1 - core], pair, 0, sibling)
    for k in (2, 1, 3):
        send(query.at[px, run], query.at[px, run], 1, along(k))
    for k in (2, 1, 3):
        send(hess.at[py], hess.at[py], 2, beside(k))
    arrived(pair, 0)
    chip = rows[core] + pair[...]
    halves = [chip[: HALF // 2], chip[HALF // 2 :]]
    for step in range(2):
        for half in range(2):
            slot = 2 * step + half
            codes[slot], scales[slot] = encode(halves[half])
            partner_group = lax.rem(group + 1 + 2 * lax.rem(group + slot // 2 + half, 2), RUNS)
            device = at(run, plane, partner_group, core)
            send(codes.at[slot], codes_in.at[slot], 10 + slot, device)
            send(scales.at[slot], scales_in.at[slot], 14 + slot, device)
        if step == 0:
            arrived(query.at[0, pl.ds(0, RUNS - 1)], 1)
            for k in (8, 4, 12):
                send(query.at[px], query.at[px], 3, beside(k))
            for half in range(2):
                arrived(codes.at[half], 10 + half)
                arrived(scales.at[half], 14 + half)
                halves[half] = halves[half] + decode(codes_in[half], scales_in[half])

    arrived(query.at[pl.ds(0, 3)], 3)
    arrived(hess.at[pl.ds(0, 3)], 2)
    contract = (((1,), (1,)), ((), ()))
    rows_of_hess = hess[...].reshape(4 * RANK, 512)

    def times(which):
        some = query[pl.ds(which * 2, 2)].reshape(HALF, 512)
        return lax.dot_general(some, rows_of_hess, contract, preferred_element_type=jnp.float32)

    product[...] = times(1 - core)
    send(product, others, 4, sibling)
    own = times(core)
    arrived(others, 4)
    both = (own + others[...]).astype(jnp.bfloat16).reshape(2, RUNS, 16, 4 * RANK)
    for k in range(RUNS):
        summed[k] = both[:, k]
    for k in (2, 1, 3):
        send(summed.at[lax.rem(group + k, RUNS)], blocks.at[k - 1], 5, across(k))

    for half in range(2):
        arrived(codes.at[2 + half], 12 + half)
        arrived(scales.at[2 + half], 16 + half)
        halves[half] = halves[half] + decode(codes_in[2 + half], scales_in[2 + half])
    whole = jnp.concatenate(halves, axis=0)
    outer = lax.dot_general(
        whole, whole, (((0,), (0,)), ((), ())),
        precision=lax.Precision.HIGHEST, preferred_element_type=jnp.float32,
    )
    partial[...] = outer[RANK:]
    send(partial, partner, 6, sibling)
    arrived(partner, 6)
    rounded = (partial[...] + partner[...]).astype(jnp.bfloat16)
    def iota(rows_, lanes, axis):
        return lax.broadcasted_iota(jnp.int32, (rows_, lanes), axis)

    def matrix(condition):
        return jnp.where(condition, 1.0, 0.0).astype(jnp.bfloat16)

    twice = matrix(iota(2 * RANK, 2 * RANK, 0) == lax.rem(iota(2 * RANK, 2 * RANK, 1), RANK))
    doubled = jnp.dot(rounded, twice, preferred_element_type=jnp.float32)
    parity = lax.rem(iota(RANK, 2 * RANK, 0), 2) == lax.div(iota(RANK, 2 * RANK, 1), RANK)
    doubled = jnp.where(parity, doubled, 0.0).astype(jnp.bfloat16)
    to, come = iota(32, RANK, 0), iota(32, RANK, 1)
    order = matrix(
        jnp.logical_and(
            lax.div(to, 8) == lax.rem(lax.div(come, 4), 4),
            lax.rem(to, 8) == lax.div(come, 16) * 2 + lax.div(lax.rem(come, 4), 2),
        )
    )
    ordered = jnp.dot(order, doubled, preferred_element_type=jnp.float32)
    factor[...] = ordered.reshape(4, 8, 2 * RANK)
    for k in PLANE:
        send(factor.at[lax.rem(px + k // 4, 4)], factors.at[plane], 7, beside(k))
    factors[plane] = factor[px]

    arrived(blocks, 5)
    b = blocks[...].astype(jnp.float32)
    gathered[run] = (summed[group].astype(jnp.float32) + b[0] + (b[1] + b[2])).astype(jnp.bfloat16)
    for k in (2, 1, 3):
        send(gathered.at[run], gathered.at[run], 8, along(k))
    arrived(factors.at[pl.ds(0, NEAR - 1)], 7)
    left_side = factors[...].reshape(NEAR * 8, 2 * RANK).astype(jnp.bfloat16)
    which = lax.rem(iota(NEAR * 8, HALF, 0), 8)
    arrived(gathered.at[pl.ds(0, RUNS - 1)], 8)
    scores = jnp.zeros((NEAR * 8, HALF), jnp.float32)
    for k in range(2 * RUNS):
        piece = gathered[k // 2, :, :, (k % 2) * 128 : (k % 2) * 128 + 128]
        right_side = jnp.concatenate([piece[0]] * 4 + [piece[1]] * 4, axis=0)
        term = lax.dot_general(left_side, right_side, contract, preferred_element_type=jnp.float32)
        scores += jnp.where(which == k, term, 0.0)
    mine = lax.div(lax.rem(iota(NEAR * 8, HALF, 1), 64), 16) == py
    scores = jnp.where(mine, scores, 0.0)
    part[...] = scores.reshape(NEAR, 8, HALF)
    for k in PLANE:
        there = lax.rem(px + k // 4, 4) * 4 + lax.rem(py + k % 4, 4)
        send(part.at[there], parts.at[plane], 9, beside(k))
    parts[plane] = part[plane]

    left(pair, 0)
    left(query.at[0, pl.ds(0, RUNS - 1)], 1)
    left(hess.at[pl.ds(0, 3)], 2)
    left(query.at[pl.ds(0, 3)], 3)
    for slot in range(4):
        left(codes.at[slot], 10 + slot)
        left(scales.at[slot], 14 + slot)
    left(others, 4)
    left(partner, 6)
    left(factors.at[pl.ds(0, NEAR - 1)], 7)
    left(gathered.at[pl.ds(0, RUNS - 1)], 8)
    left(blocks, 5)
    arrived(parts.at[pl.ds(0, NEAR - 1)], 9)
    total = jnp.sum(parts[...], axis=0)
    out[...] = jnp.sum(total, axis=0, keepdims=True)
    left(parts.at[pl.ds(0, NEAR - 1)], 9)


def on_device(activations, output_grads, projection, token_counts, hessian_inverse, queries):
    anywhere = pl.BlockSpec(memory_space=pltpu.HBM)
    bf16, f32 = jnp.bfloat16, jnp.float32
    scratch = [
        pltpu.VMEM((1, 256, 1024), bf16),
        pltpu.VMEM((1, 256, 1024), bf16),
        pltpu.VMEM((1024, 128), bf16),
        pltpu.SMEM((1,), jnp.int32),
        pltpu.VMEM((2, HALF, 128), f32),
        pltpu.VMEM((HALF, 128), f32),
        pltpu.VMEM((4, HALF // 2, 128), jnp.int16),
        pltpu.VMEM((4, HALF // 2, 128), jnp.int16),
        pltpu.VMEM((4, 8, 128), f32),
        pltpu.VMEM((4, 8, 128), f32),
        pltpu.VMEM((RANK, 128), f32),
        pltpu.VMEM((RANK, 128), f32),
        pltpu.VMEM((4, 8, 128), f32),
        pltpu.VMEM((NEAR, 8, 128), f32),
        pltpu.VMEM((4, RANK, 512), bf16),
        pltpu.VMEM((4, RUNS, 16, 512), bf16),
        pltpu.VMEM((HALF, 4 * RANK), f32),
        pltpu.VMEM((HALF, 4 * RANK), f32),
        pltpu.VMEM((RUNS, 2, 16, 4 * RANK), bf16),
        pltpu.VMEM((RUNS - 1, 2, 16, 4 * RANK), bf16),
        pltpu.VMEM((RUNS, 2, 16, 4 * RANK), bf16),
        pltpu.VMEM((NEAR, 8, HALF), f32),
        pltpu.VMEM((NEAR, 8, HALF), f32),
        pltpu.SemaphoreType.DMA((6,)),
        pltpu.SemaphoreType.DMA((18,)),
        pltpu.SemaphoreType.DMA((18,)),
    ]
    return pl.pallas_call(
        attribute,
        out_shape=jax.ShapeDtypeStruct((1, HALF), f32),
        in_specs=[anywhere] * 6,
        out_specs=pl.BlockSpec(memory_space=pltpu.VMEM),
        scratch_shapes=scratch,
        compiler_params=pltpu.CompilerParams(
            collective_id=0, has_side_effects=True, vmem_limit_bytes=60 << 20
        ),
        cost_estimate=pl.CostEstimate(flops=200_000_000, bytes_accessed=1_500_000, transcendentals=0),
        name="attribute",
    )(activations, output_grads, projection, token_counts, hessian_inverse, queries)


def solution(mesh):
    placed = (
        P("dp", None, "tensor"),
        P("dp", None, "tensor"),
        P("tensor", None),
        P("dp"),
        P("dp", "tensor"),
        P("dp", "tensor"),
    )
    return jax.shard_map(
        on_device, mesh=mesh, in_specs=placed, out_specs=P("dp", "tensor"), check_vma=False
    )
```

```python
import jax
import jax.numpy as jnp
from jax import lax
from jax.experimental import pallas as pl
from jax.experimental.pallas import tpu as pltpu
from jax.sharding import PartitionSpec as P

MESH = pl.DeviceIdType.MESH
NEAR = 16
RUNS = 4
RANK = 64
HALF = 128
PLANE = sorted(range(1, NEAR), key=lambda k: -(min(k // 4, 4 - k // 4) + min(k % 4, 4 - k % 4)))


def encode(values):
    most = jnp.maximum(jnp.max(jnp.abs(values), axis=0, keepdims=True), 1e-30)
    codes = jnp.round(values * (32000.0 / most)).astype(jnp.int32).astype(jnp.int16)
    return codes, jnp.broadcast_to(most * (1.0 / 32000.0), (8, 128))


def decode(codes, scales):
    return codes.astype(jnp.int32).astype(jnp.float32) * scales[:1]


def attribute(
    acts_hbm, grads_hbm, proj_hbm, counts_hbm, hess_hbm, query_hbm, out,
    acts, grads, proj, counts, rows, pair, codes, codes_in, scales, scales_in, partial, partner, factor, factors,
    hess, query, product, others, summed, blocks, gathered, part, parts,
    load_sem, send_sem, recv_sem, piece_sem,
):
    d, s = lax.axis_index("dp"), lax.axis_index("tensor")
    run, plane = d // NEAR, lax.rem(d, NEAR)
    px, py = plane // 4, lax.rem(plane, 4)
    group, core = s // 2, lax.rem(s, 2)

    def at(run_, plane_, group_, core_):
        return (run_ * NEAR + plane_, group_ * 2 + core_)

    def beside(k):
        return at(run, lax.rem(px + k // 4, 4) * 4 + lax.rem(py + k % 4, 4), group, core)

    def along(k):
        return at(lax.rem(run + k, RUNS), plane, group, core)

    def across(k):
        return at(run, plane, lax.rem(group + k, RUNS), core)

    sibling = at(run, plane, group, 1 - core)

    def send(src, dst, k, device):
        pltpu.make_async_remote_copy(
            src, dst, send_sem.at[k], recv_sem.at[k], device_id=device, device_id_type=MESH
        ).start()

    def arrived(ref, k):
        pltpu.make_async_copy(ref, ref, recv_sem.at[k]).wait()

    def left(ref, k):
        pltpu.make_async_copy(ref, ref, send_sem.at[k]).wait()

    barrier = pltpu.get_barrier_semaphore()
    greeted = [across(1), across(3)] + [along(k) for k in (2, 1, 3)] + [beside(k) for k in (8, 2, 4, 12, 1, 3)] + [sibling]
    for device in greeted:
        pl.semaphore_signal(barrier, inc=1, device_id=device, device_id_type=MESH)
    loads = [
        pltpu.make_async_copy(query_hbm, query.at[px, run], load_sem.at[0]),
        pltpu.make_async_copy(hess_hbm, hess.at[py], load_sem.at[1]),
        pltpu.make_async_copy(proj_hbm, proj, load_sem.at[2]),
        pltpu.make_async_copy(acts_hbm, acts, load_sem.at[3]),
        pltpu.make_async_copy(grads_hbm, grads, load_sem.at[4]),
        pltpu.make_async_copy(counts_hbm, counts, load_sem.at[5]),
    ]
    for load in loads:
        load.start()

    for load in loads[2:]:
        load.wait()
    lane = lax.broadcasted_iota(jnp.int32, (2 * HALF, 2 * RANK), 1)
    position = lax.broadcasted_iota(jnp.int32, (2 * HALF, 2 * RANK), 0)
    inputs_side = jnp.dot(acts[0], proj[...], preferred_element_type=jnp.float32)
    output_side = jnp.dot(grads[0], proj[...], preferred_element_type=jnp.float32)
    projected = jnp.where(lane < RANK, inputs_side, output_side)
    projected = jnp.where(position < counts[0], projected, 0.0)
    rows[0] = projected[:HALF]
    rows[1] = projected[HALF:]
    for load in loads[:2]:
        load.wait()

    pl.semaphore_wait(barrier, len(greeted))
    send(rows.at[1 - core], pair, 0, sibling)
    for k in (1, 2, 3):
        pltpu.make_async_remote_copy(
            query.at[px, run], query.at[px, run], send_sem.at[1], piece_sem.at[RUNS - k - 1],
            device_id=along(k), device_id_type=MESH,
        ).start()
    for k in (8, 4, 12):
        send(query.at[px, run], query.at[px, run], 3, beside(k))
    for k in (2, 1, 3):
        send(hess.at[py], hess.at[py], 2, beside(k))
    arrived(pair, 0)
    chip = rows[core] + pair[...]
    halves = [chip[: HALF // 2], chip[HALF // 2 :]]
    def exchange(step):
        for half in range(2):
            slot = 2 * step + half
            codes[slot], scales[slot] = encode(halves[half])
            partner_group = lax.rem(group + 1 + 2 * lax.rem(group + slot // 2 + half, 2), RUNS)
            device = at(run, plane, partner_group, core)
            send(codes.at[slot], codes_in.at[slot], 10 + slot, device)
            send(scales.at[slot], scales_in.at[slot], 14 + slot, device)

    exchange(0)
    first = jnp.where(run == 3, 3, 1)
    second = jnp.where(jnp.logical_or(run == 0, run == 3), 2, 3)
    for k in (first, second, 6 - first - second):
        there = lax.rem(run + k, RUNS)
        pltpu.make_async_copy(query.at[px, there], query.at[px, there], piece_sem.at[k - 1]).wait()
        for j in (8, 4, 12):
            send(query.at[px, there], query.at[px, there], 3, beside(j))

    for half in range(2):
        arrived(codes.at[half], 10 + half)
        arrived(scales.at[half], 14 + half)
        halves[half] = halves[half] + decode(codes_in[half], scales_in[half])
    exchange(1)

    arrived(query.at[pl.ds(0, 3)], 3)
    arrived(hess.at[pl.ds(0, 3)], 2)
    contract = (((1,), (1,)), ((), ()))
    rows_of_hess = hess[...].reshape(4 * RANK, 512)

    def times(which):
        some = query[pl.ds(which * 2, 2)].reshape(HALF, 512)
        return lax.dot_general(some, rows_of_hess, contract, preferred_element_type=jnp.float32)

    product[...] = times(1 - core)
    send(product, others, 4, sibling)
    own = times(core)
    arrived(others, 4)
    both = (own + others[...]).astype(jnp.bfloat16).reshape(2, RUNS, 16, 4 * RANK)
    for k in range(RUNS):
        summed[k] = both[:, k]
    for k in (2, 1, 3):
        send(summed.at[lax.rem(group + k, RUNS)], blocks.at[k - 1], 5, across(k))

    for half in range(2):
        arrived(codes.at[2 + half], 12 + half)
        arrived(scales.at[2 + half], 16 + half)
        halves[half] = halves[half] + decode(codes_in[2 + half], scales_in[2 + half])
    whole = jnp.concatenate(halves, axis=0)
    outer = lax.dot_general(
        whole, whole, (((0,), (0,)), ((), ())),
        precision=lax.Precision.HIGHEST, preferred_element_type=jnp.float32,
    )
    partial[...] = outer[RANK:]
    send(partial, partner, 6, sibling)
    arrived(partner, 6)
    rounded = (partial[...] + partner[...]).astype(jnp.bfloat16)
    def iota(rows_, lanes, axis):
        return lax.broadcasted_iota(jnp.int32, (rows_, lanes), axis)

    def matrix(condition):
        return jnp.where(condition, 1.0, 0.0).astype(jnp.bfloat16)

    twice = matrix(iota(2 * RANK, 2 * RANK, 0) == lax.rem(iota(2 * RANK, 2 * RANK, 1), RANK))
    doubled = jnp.dot(rounded, twice, preferred_element_type=jnp.float32)
    parity = lax.rem(iota(RANK, 2 * RANK, 0), 2) == lax.div(iota(RANK, 2 * RANK, 1), RANK)
    doubled = jnp.where(parity, doubled, 0.0).astype(jnp.bfloat16)
    to, come = iota(32, RANK, 0), iota(32, RANK, 1)
    order = matrix(
        jnp.logical_and(
            lax.div(to, 8) == lax.rem(lax.div(come, 4), 4),
            lax.rem(to, 8) == lax.div(come, 16) * 2 + lax.div(lax.rem(come, 4), 2),
        )
    )
    ordered = jnp.dot(order, doubled, preferred_element_type=jnp.float32)
    factor[...] = ordered.reshape(4, 8, 2 * RANK)
    for k in PLANE:
        send(factor.at[lax.rem(px + k // 4, 4)], factors.at[plane], 7, beside(k))
    factors[plane] = factor[px]

    arrived(blocks, 5)
    b = blocks[...].astype(jnp.float32)
    gathered[run] = (summed[group].astype(jnp.float32) + b[0] + (b[1] + b[2])).astype(jnp.bfloat16)
    for k in (2, 1, 3):
        send(gathered.at[run], gathered.at[run], 8, along(k))
    arrived(factors.at[pl.ds(0, NEAR - 1)], 7)
    left_side = factors[...].reshape(NEAR * 8, 2 * RANK).astype(jnp.bfloat16)
    which = lax.rem(iota(NEAR * 8, HALF, 0), 8)
    arrived(gathered.at[pl.ds(0, RUNS - 1)], 8)
    scores = jnp.zeros((NEAR * 8, HALF), jnp.float32)
    for k in range(2 * RUNS):
        piece = gathered[k // 2, :, :, (k % 2) * 128 : (k % 2) * 128 + 128]
        right_side = jnp.concatenate([piece[0]] * 4 + [piece[1]] * 4, axis=0)
        term = lax.dot_general(left_side, right_side, contract, preferred_element_type=jnp.float32)
        scores += jnp.where(which == k, term, 0.0)
    mine = lax.div(lax.rem(iota(NEAR * 8, HALF, 1), 64), 16) == py
    scores = jnp.where(mine, scores, 0.0)
    part[...] = scores.reshape(NEAR, 8, HALF)
    for k in PLANE:
        there = lax.rem(px + k // 4, 4) * 4 + lax.rem(py + k % 4, 4)
        send(part.at[there], parts.at[plane], 9, beside(k))
    parts[plane] = part[plane]

    left(pair, 0)
    left(query.at[0, pl.ds(0, RUNS - 1)], 1)
    left(hess.at[pl.ds(0, 3)], 2)
    left(query.at[pl.ds(0, 3)], 3)
    for slot in range(4):
        left(codes.at[slot], 10 + slot)
        left(scales.at[slot], 14 + slot)
    left(others, 4)
    left(partner, 6)
    left(factors.at[pl.ds(0, NEAR - 1)], 7)
    left(gathered.at[pl.ds(0, RUNS - 1)], 8)
    left(blocks, 5)
    arrived(parts.at[pl.ds(0, NEAR - 1)], 9)
    total = jnp.sum(parts[...], axis=0)
    out[...] = jnp.sum(total, axis=0, keepdims=True)
    left(parts.at[pl.ds(0, NEAR - 1)], 9)


def on_device(activations, output_grads, projection, token_counts, hessian_inverse, queries):
    anywhere = pl.BlockSpec(memory_space=pltpu.HBM)
    bf16, f32 = jnp.bfloat16, jnp.float32
    scratch = [
        pltpu.VMEM((1, 256, 1024), bf16),
        pltpu.VMEM((1, 256, 1024), bf16),
        pltpu.VMEM((1024, 128), bf16),
        pltpu.SMEM((1,), jnp.int32),
        pltpu.VMEM((2, HALF, 128), f32),
        pltpu.VMEM((HALF, 128), f32),
        pltpu.VMEM((4, HALF // 2, 128), jnp.int16),
        pltpu.VMEM((4, HALF // 2, 128), jnp.int16),
        pltpu.VMEM((4, 8, 128), f32),
        pltpu.VMEM((4, 8, 128), f32),
        pltpu.VMEM((RANK, 128), f32),
        pltpu.VMEM((RANK, 128), f32),
        pltpu.VMEM((4, 8, 128), f32),
        pltpu.VMEM((NEAR, 8, 128), f32),
        pltpu.VMEM((4, RANK, 512), bf16),
        pltpu.VMEM((4, RUNS, 16, 512), bf16),
        pltpu.VMEM((HALF, 4 * RANK), f32),
        pltpu.VMEM((HALF, 4 * RANK), f32),
        pltpu.VMEM((RUNS, 2, 16, 4 * RANK), bf16),
        pltpu.VMEM((RUNS - 1, 2, 16, 4 * RANK), bf16),
        pltpu.VMEM((RUNS, 2, 16, 4 * RANK), bf16),
        pltpu.VMEM((NEAR, 8, HALF), f32),
        pltpu.VMEM((NEAR, 8, HALF), f32),
        pltpu.SemaphoreType.DMA((6,)),
        pltpu.SemaphoreType.DMA((18,)),
        pltpu.SemaphoreType.DMA((18,)),
        pltpu.SemaphoreType.DMA((RUNS - 1,)),
    ]
    return pl.pallas_call(
        attribute,
        out_shape=jax.ShapeDtypeStruct((1, HALF), f32),
        in_specs=[anywhere] * 6,
        out_specs=pl.BlockSpec(memory_space=pltpu.VMEM),
        scratch_shapes=scratch,
        compiler_params=pltpu.CompilerParams(
            collective_id=0, has_side_effects=True, vmem_limit_bytes=60 << 20
        ),
        cost_estimate=pl.CostEstimate(flops=200_000_000, bytes_accessed=1_500_000, transcendentals=0),
        name="attribute",
    )(activations, output_grads, projection, token_counts, hessian_inverse, queries)


def solution(mesh):
    placed = (
        P("dp", None, "tensor"),
        P("dp", None, "tensor"),
        P("tensor", None),
        P("dp"),
        P("dp", "tensor"),
        P("dp", "tensor"),
    )
    return jax.shard_map(
        on_device, mesh=mesh, in_specs=placed, out_specs=P("dp", "tensor"), check_vma=False
    )
```

```python
import jax
import jax.numpy as jnp
from jax import lax
from jax.experimental import pallas as pl
from jax.experimental.pallas import tpu as pltpu
from jax.sharding import PartitionSpec as P

MESH = pl.DeviceIdType.MESH
NEAR = 16
RUNS = 4
RANK = 64
HALF = 128
PLANE = sorted(range(1, NEAR), key=lambda k: -(min(k // 4, 4 - k // 4) + min(k % 4, 4 - k % 4)))


def encode(values):
    most = jnp.maximum(jnp.max(jnp.abs(values), axis=0, keepdims=True), 1e-30)
    codes = jnp.round(values * (32000.0 / most)).astype(jnp.int32).astype(jnp.int16)
    return codes, jnp.broadcast_to(most * (1.0 / 32000.0), (8, 128))


def decode(codes, scales):
    return codes.astype(jnp.int32).astype(jnp.float32) * scales[:1]


def attribute(
    acts_hbm, grads_hbm, proj_hbm, counts_hbm, hess_hbm, query_hbm, out,
    acts, grads, proj, counts, rows, pair, codes, codes_in, scales, scales_in, partial, partner, factor, factors,
    hess, query, product, others, ours, summed, blocks, gathered, part, parts,
    load_sem, send_sem, recv_sem, piece_sem, pair_sem,
):
    d, s = lax.axis_index("dp"), lax.axis_index("tensor")
    run, plane = d // NEAR, lax.rem(d, NEAR)
    px, py = plane // 4, lax.rem(plane, 4)
    group, core = s // 2, lax.rem(s, 2)

    def at(run_, plane_, group_, core_):
        return (run_ * NEAR + plane_, group_ * 2 + core_)

    def beside(k):
        return at(run, lax.rem(px + k // 4, 4) * 4 + lax.rem(py + k % 4, 4), group, core)

    def along(k):
        return at(lax.rem(run + k, RUNS), plane, group, core)

    def across(k):
        return at(run, plane, lax.rem(group + k, RUNS), core)

    sibling = at(run, plane, group, 1 - core)

    def send(src, dst, k, device):
        pltpu.make_async_remote_copy(
            src, dst, send_sem.at[k], recv_sem.at[k], device_id=device, device_id_type=MESH
        ).start()

    def arrived(ref, k):
        pltpu.make_async_copy(ref, ref, recv_sem.at[k]).wait()

    def left(ref, k):
        pltpu.make_async_copy(ref, ref, send_sem.at[k]).wait()

    barrier = pltpu.get_barrier_semaphore()
    greeted = [across(1), across(3)] + [along(k) for k in (2, 1, 3)] + [beside(k) for k in (8, 2, 4, 12, 1, 3)] + [sibling]
    for device in greeted:
        pl.semaphore_signal(barrier, inc=1, device_id=device, device_id_type=MESH)
    loads = [
        pltpu.make_async_copy(query_hbm, query.at[px, run], load_sem.at[0]),
        pltpu.make_async_copy(hess_hbm, hess.at[py], load_sem.at[1]),
        pltpu.make_async_copy(proj_hbm, proj, load_sem.at[2]),
        pltpu.make_async_copy(acts_hbm, acts, load_sem.at[3]),
        pltpu.make_async_copy(grads_hbm, grads, load_sem.at[4]),
        pltpu.make_async_copy(counts_hbm, counts, load_sem.at[5]),
    ]
    for load in loads:
        load.start()

    for load in loads[2:]:
        load.wait()
    lane = lax.broadcasted_iota(jnp.int32, (2 * HALF, 2 * RANK), 1)
    position = lax.broadcasted_iota(jnp.int32, (2 * HALF, 2 * RANK), 0)
    inputs_side = jnp.dot(acts[0], proj[...], preferred_element_type=jnp.float32)
    output_side = jnp.dot(grads[0], proj[...], preferred_element_type=jnp.float32)
    projected = jnp.where(lane < RANK, inputs_side, output_side)
    projected = jnp.where(position < counts[0], projected, 0.0)
    rows[0] = projected[:HALF]
    rows[1] = projected[HALF:]
    for load in loads[:2]:
        load.wait()

    pl.semaphore_wait(barrier, len(greeted))
    send(rows.at[1 - core], pair, 0, sibling)
    for k in (1, 2, 3):
        pltpu.make_async_remote_copy(
            query.at[px, run], query.at[px, run], send_sem.at[1], piece_sem.at[RUNS - k - 1],
            device_id=along(k), device_id_type=MESH,
        ).start()
    for k in (8, 4, 12):
        send(query.at[px, run], query.at[px, run], 3, beside(k))
    for k in (2, 1, 3):
        send(hess.at[py], hess.at[py], 2, beside(k))
    arrived(pair, 0)
    chip = rows[core] + pair[...]
    halves = [chip[: HALF // 2], chip[HALF // 2 :]]
    def exchange(step):
        for half in range(2):
            slot = 2 * step + half
            codes[slot], scales[slot] = encode(halves[half])
            partner_group = lax.rem(group + 1 + 2 * lax.rem(group + slot // 2 + half, 2), RUNS)
            device = at(run, plane, partner_group, core)
            send(codes.at[slot], codes_in.at[slot], 10 + slot, device)
            send(scales.at[slot], scales_in.at[slot], 14 + slot, device)

    exchange(0)
    first = jnp.where(run == 3, 3, 1)
    second = jnp.where(jnp.logical_or(run == 0, run == 3), 2, 3)
    for k in (first, second, 6 - first - second):
        there = lax.rem(run + k, RUNS)
        pltpu.make_async_copy(query.at[px, there], query.at[px, there], piece_sem.at[k - 1]).wait()
        for j in (8, 4, 12):
            send(query.at[px, there], query.at[px, there], 3, beside(j))

    for half in range(2):
        arrived(codes.at[half], 10 + half)
        arrived(scales.at[half], 14 + half)
        halves[half] = halves[half] + decode(codes_in[half], scales_in[half])
    exchange(1)

    arrived(query.at[pl.ds(0, 3)], 3)
    arrived(hess.at[pl.ds(0, 3)], 2)
    contract = (((1,), (1,)), ((), ()))
    rows_of_hess = hess[...].reshape(4 * RANK, 512)

    def times(which):
        some = query[pl.ds(which * 2, 2)].reshape(HALF, 512)
        return lax.dot_general(some, rows_of_hess, contract, preferred_element_type=jnp.float32)

    def by_run(which):
        return times(which).reshape(2, RUNS, 16, 4 * RANK)

    away = [lax.rem(group + k, RUNS) for k in (2, 1, 3, 0)]
    theirs = by_run(1 - core)
    for k in range(RUNS):
        product[k] = theirs[:, k]
    for k in away:
        pltpu.make_async_remote_copy(
            product.at[k], others.at[k], send_sem.at[4], pair_sem.at[k], device_id=sibling, device_id_type=MESH
        ).start()
    own = by_run(core)
    for k in range(RUNS):
        ours[k] = own[:, k]
    for place, k in enumerate(away):
        pltpu.make_async_copy(others.at[k], others.at[k], pair_sem.at[k]).wait()
        summed[k] = (ours[k] + others[k]).astype(jnp.bfloat16)
        if place < RUNS - 1:
            apart = (2, 1, 3)[place]
            send(summed.at[k], blocks.at[apart - 1], 5, across(apart))

    for half in range(2):
        arrived(codes.at[2 + half], 12 + half)
        arrived(scales.at[2 + half], 16 + half)
        halves[half] = halves[half] + decode(codes_in[2 + half], scales_in[2 + half])
    whole = jnp.concatenate(halves, axis=0)
    outer = lax.dot_general(
        whole, whole, (((0,), (0,)), ((), ())),
        precision=lax.Precision.HIGHEST, preferred_element_type=jnp.float32,
    )
    partial[...] = outer[RANK:]
    send(partial, partner, 6, sibling)
    arrived(partner, 6)
    rounded = (partial[...] + partner[...]).astype(jnp.bfloat16)
    def iota(rows_, lanes, axis):
        return lax.broadcasted_iota(jnp.int32, (rows_, lanes), axis)

    def matrix(condition):
        return jnp.where(condition, 1.0, 0.0).astype(jnp.bfloat16)

    twice = matrix(iota(2 * RANK, 2 * RANK, 0) == lax.rem(iota(2 * RANK, 2 * RANK, 1), RANK))
    doubled = jnp.dot(rounded, twice, preferred_element_type=jnp.float32)
    parity = lax.rem(iota(RANK, 2 * RANK, 0), 2) == lax.div(iota(RANK, 2 * RANK, 1), RANK)
    doubled = jnp.where(parity, doubled, 0.0).astype(jnp.bfloat16)
    to, come = iota(32, RANK, 0), iota(32, RANK, 1)
    order = matrix(
        jnp.logical_and(
            lax.div(to, 8) == lax.rem(lax.div(come, 4), 4),
            lax.rem(to, 8) == lax.div(come, 16) * 2 + lax.div(lax.rem(come, 4), 2),
        )
    )
    ordered = jnp.dot(order, doubled, preferred_element_type=jnp.float32)
    factor[...] = ordered.reshape(4, 8, 2 * RANK)
    for k in PLANE:
        send(factor.at[lax.rem(px + k // 4, 4)], factors.at[plane], 7, beside(k))
    factors[plane] = factor[px]

    arrived(blocks, 5)
    b = blocks[...].astype(jnp.float32)
    gathered[run] = (summed[group].astype(jnp.float32) + b[0] + (b[1] + b[2])).astype(jnp.bfloat16)
    for k in (2, 1, 3):
        send(gathered.at[run], gathered.at[run], 8, along(k))
    arrived(factors.at[pl.ds(0, NEAR - 1)], 7)
    left_side = factors[...].reshape(NEAR * 8, 2 * RANK).astype(jnp.bfloat16)
    which = lax.rem(iota(NEAR * 8, HALF, 0), 8)
    arrived(gathered.at[pl.ds(0, RUNS - 1)], 8)
    scores = jnp.zeros((NEAR * 8, HALF), jnp.float32)
    for k in range(2 * RUNS):
        piece = gathered[k // 2, :, :, (k % 2) * 128 : (k % 2) * 128 + 128]
        right_side = jnp.concatenate([piece[0]] * 4 + [piece[1]] * 4, axis=0)
        term = lax.dot_general(left_side, right_side, contract, preferred_element_type=jnp.float32)
        scores += jnp.where(which == k, term, 0.0)
    mine = lax.div(lax.rem(iota(NEAR * 8, HALF, 1), 64), 16) == py
    scores = jnp.where(mine, scores, 0.0)
    part[...] = scores.reshape(NEAR, 8, HALF)
    for k in PLANE:
        there = lax.rem(px + k // 4, 4) * 4 + lax.rem(py + k % 4, 4)
        send(part.at[there], parts.at[plane], 9, beside(k))
    parts[plane] = part[plane]

    left(pair, 0)
    left(query.at[0, pl.ds(0, RUNS - 1)], 1)
    left(hess.at[pl.ds(0, 3)], 2)
    left(query.at[pl.ds(0, 3)], 3)
    for slot in range(4):
        left(codes.at[slot], 10 + slot)
        left(scales.at[slot], 14 + slot)
    left(others, 4)
    left(partner, 6)
    left(factors.at[pl.ds(0, NEAR - 1)], 7)
    left(gathered.at[pl.ds(0, RUNS - 1)], 8)
    left(blocks, 5)
    arrived(parts.at[pl.ds(0, NEAR - 1)], 9)
    total = jnp.sum(parts[...], axis=0)
    out[...] = jnp.sum(total, axis=0, keepdims=True)
    left(parts.at[pl.ds(0, NEAR - 1)], 9)


def on_device(activations, output_grads, projection, token_counts, hessian_inverse, queries):
    anywhere = pl.BlockSpec(memory_space=pltpu.HBM)
    bf16, f32 = jnp.bfloat16, jnp.float32
    scratch = [
        pltpu.VMEM((1, 256, 1024), bf16),
        pltpu.VMEM((1, 256, 1024), bf16),
        pltpu.VMEM((1024, 128), bf16),
        pltpu.SMEM((1,), jnp.int32),
        pltpu.VMEM((2, HALF, 128), f32),
        pltpu.VMEM((HALF, 128), f32),
        pltpu.VMEM((4, HALF // 2, 128), jnp.int16),
        pltpu.VMEM((4, HALF // 2, 128), jnp.int16),
        pltpu.VMEM((4, 8, 128), f32),
        pltpu.VMEM((4, 8, 128), f32),
        pltpu.VMEM((RANK, 128), f32),
        pltpu.VMEM((RANK, 128), f32),
        pltpu.VMEM((4, 8, 128), f32),
        pltpu.VMEM((NEAR, 8, 128), f32),
        pltpu.VMEM((4, RANK, 512), bf16),
        pltpu.VMEM((4, RUNS, 16, 512), bf16),
        pltpu.VMEM((RUNS, 2, 16, 4 * RANK), f32),
        pltpu.VMEM((RUNS, 2, 16, 4 * RANK), f32),
        pltpu.VMEM((RUNS, 2, 16, 4 * RANK), f32),
        pltpu.VMEM((RUNS, 2, 16, 4 * RANK), bf16),
        pltpu.VMEM((RUNS - 1, 2, 16, 4 * RANK), bf16),
        pltpu.VMEM((RUNS, 2, 16, 4 * RANK), bf16),
        pltpu.VMEM((NEAR, 8, HALF), f32),
        pltpu.VMEM((NEAR, 8, HALF), f32),
        pltpu.SemaphoreType.DMA((6,)),
        pltpu.SemaphoreType.DMA((18,)),
        pltpu.SemaphoreType.DMA((18,)),
        pltpu.SemaphoreType.DMA((RUNS - 1,)),
        pltpu.SemaphoreType.DMA((RUNS,)),
    ]
    return pl.pallas_call(
        attribute,
        out_shape=jax.ShapeDtypeStruct((1, HALF), f32),
        in_specs=[anywhere] * 6,
        out_specs=pl.BlockSpec(memory_space=pltpu.VMEM),
        scratch_shapes=scratch,
        compiler_params=pltpu.CompilerParams(
            collective_id=0, has_side_effects=True, vmem_limit_bytes=60 << 20
        ),
        cost_estimate=pl.CostEstimate(flops=200_000_000, bytes_accessed=1_500_000, transcendentals=0),
        name="attribute",
    )(activations, output_grads, projection, token_counts, hessian_inverse, queries)


def solution(mesh):
    placed = (
        P("dp", None, "tensor"),
        P("dp", None, "tensor"),
        P("tensor", None),
        P("dp"),
        P("dp", "tensor"),
        P("dp", "tensor"),
    )
    return jax.shard_map(
        on_device, mesh=mesh, in_specs=placed, out_specs=P("dp", "tensor"), check_vma=False
    )
```

```python
import jax
import jax.numpy as jnp
from jax import lax
from jax.experimental import pallas as pl
from jax.experimental.pallas import tpu as pltpu
from jax.sharding import PartitionSpec as P

MESH = pl.DeviceIdType.MESH
NEAR = 16
RUNS = 4
RANK = 64
HALF = 128
PLANE = sorted(range(1, NEAR), key=lambda k: -(min(k // 4, 4 - k // 4) + min(k % 4, 4 - k % 4)))


def encode(values):
    most = jnp.maximum(jnp.max(jnp.abs(values), axis=0, keepdims=True), 1e-30)
    codes = jnp.round(values * (32000.0 / most)).astype(jnp.int32).astype(jnp.int16)
    return codes, jnp.broadcast_to(most * (1.0 / 32000.0), (8, 128))


def decode(codes, scales):
    return codes.astype(jnp.int32).astype(jnp.float32) * scales[:1]


def attribute(
    acts_hbm, grads_hbm, proj_hbm, counts_hbm, hess_hbm, query_hbm, out,
    acts, grads, proj, counts, rows, pair, codes, codes_in, scales, scales_in, partial, partner, factor, factors,
    hess, query, product, others, ours, summed, blocks, gathered, part, parts,
    load_sem, send_sem, recv_sem, piece_sem, pair_sem,
):
    d, s = lax.axis_index("dp"), lax.axis_index("tensor")
    run, plane = d // NEAR, lax.rem(d, NEAR)
    px, py = plane // 4, lax.rem(plane, 4)
    group, core = s // 2, lax.rem(s, 2)

    def at(run_, plane_, group_, core_):
        return (run_ * NEAR + plane_, group_ * 2 + core_)

    def beside(k):
        return at(run, lax.rem(px + k // 4, 4) * 4 + lax.rem(py + k % 4, 4), group, core)

    def along(k):
        return at(lax.rem(run + k, RUNS), plane, group, core)

    def across(k):
        return at(run, plane, lax.rem(group + k, RUNS), core)

    sibling = at(run, plane, group, 1 - core)

    def send(src, dst, k, device):
        pltpu.make_async_remote_copy(
            src, dst, send_sem.at[k], recv_sem.at[k], device_id=device, device_id_type=MESH
        ).start()

    def arrived(ref, k):
        pltpu.make_async_copy(ref, ref, recv_sem.at[k]).wait()

    def left(ref, k):
        pltpu.make_async_copy(ref, ref, send_sem.at[k]).wait()

    barrier = pltpu.get_barrier_semaphore()
    greeted = [across(1), across(3)] + [along(k) for k in (2, 1, 3)] + [beside(k) for k in (8, 2, 4, 12, 1, 3)] + [sibling]
    for device in greeted:
        pl.semaphore_signal(barrier, inc=1, device_id=device, device_id_type=MESH)
    loads = [
        pltpu.make_async_copy(query_hbm, query.at[px, run], load_sem.at[0]),
        pltpu.make_async_copy(hess_hbm, hess.at[py], load_sem.at[1]),
        pltpu.make_async_copy(proj_hbm, proj, load_sem.at[2]),
        pltpu.make_async_copy(acts_hbm, acts, load_sem.at[3]),
        pltpu.make_async_copy(grads_hbm, grads, load_sem.at[4]),
        pltpu.make_async_copy(counts_hbm, counts, load_sem.at[5]),
    ]
    for load in loads:
        load.start()

    for load in loads[2:]:
        load.wait()
    lane = lax.broadcasted_iota(jnp.int32, (2 * HALF, 2 * RANK), 1)
    position = lax.broadcasted_iota(jnp.int32, (2 * HALF, 2 * RANK), 0)
    inputs_side = jnp.dot(acts[0], proj[...], preferred_element_type=jnp.float32)
    output_side = jnp.dot(grads[0], proj[...], preferred_element_type=jnp.float32)
    projected = jnp.where(lane < RANK, inputs_side, output_side)
    projected = jnp.where(position < counts[0], projected, 0.0)
    rows[0] = projected[:HALF]
    rows[1] = projected[HALF:]
    for load in loads[:2]:
        load.wait()

    pl.semaphore_wait(barrier, len(greeted))
    send(rows.at[1 - core], pair, 0, sibling)
    for k in (1, 2, 3):
        pltpu.make_async_remote_copy(
            query.at[px, run], query.at[px, run], send_sem.at[1], piece_sem.at[RUNS - k - 1],
            device_id=along(k), device_id_type=MESH,
        ).start()
    for k in (8, 4, 12):
        send(query.at[px, run], query.at[px, run], 3, beside(k))
    for k in (2, 1, 3):
        send(hess.at[py], hess.at[py], 2, beside(k))
    arrived(pair, 0)
    chip = rows[core] + pair[...]
    halves = [chip[: HALF // 2], chip[HALF // 2 :]]
    def exchange(step):
        for half in range(2):
            slot = 2 * step + half
            codes[slot], scales[slot] = encode(halves[half])
            partner_group = lax.rem(group + 1 + 2 * lax.rem(group + slot // 2 + half, 2), RUNS)
            device = at(run, plane, partner_group, core)
            send(codes.at[slot], codes_in.at[slot], 10 + slot, device)
            send(scales.at[slot], scales_in.at[slot], 14 + slot, device)

    exchange(0)
    first = jnp.where(run == 3, 3, 1)
    second = jnp.where(jnp.logical_or(run == 0, run == 3), 2, 3)
    for k in (first, second, 6 - first - second):
        there = lax.rem(run + k, RUNS)
        pltpu.make_async_copy(query.at[px, there], query.at[px, there], piece_sem.at[k - 1]).wait()
        for j in (8, 4, 12):
            send(query.at[px, there], query.at[px, there], 3, beside(j))

    for half in range(2):
        arrived(codes.at[half], 10 + half)
        arrived(scales.at[half], 14 + half)
        halves[half] = halves[half] + decode(codes_in[half], scales_in[half])
    exchange(1)

    arrived(query.at[pl.ds(0, 3)], 3)
    arrived(hess.at[pl.ds(0, 3)], 2)
    contract = (((1,), (1,)), ((), ()))
    rows_of_hess = hess[...].reshape(4 * RANK, 512)

    def times(which):
        some = query[pl.ds(which * 2, 2)].reshape(HALF, 512)
        return lax.dot_general(some, rows_of_hess, contract, preferred_element_type=jnp.float32)

    def by_run(which):
        return times(which).reshape(2, RUNS, 16, 4 * RANK)

    away = [lax.rem(group + k, RUNS) for k in (2, 1, 3, 0)]
    theirs = by_run(1 - core)
    for k in range(RUNS):
        product[k] = theirs[:, k]
    for k in away:
        pltpu.make_async_remote_copy(
            product.at[k], others.at[k], send_sem.at[4], pair_sem.at[k], device_id=sibling, device_id_type=MESH
        ).start()
    own = by_run(core)
    for k in range(RUNS):
        ours[k] = own[:, k]
    for place, k in enumerate(away):
        pltpu.make_async_copy(others.at[k], others.at[k], pair_sem.at[k]).wait()
        summed[k] = (ours[k] + others[k]).astype(jnp.bfloat16)
        if place < RUNS - 1:
            apart = (2, 1, 3)[place]
            send(summed.at[k], blocks.at[apart - 1], 5, across(apart))

    for half in range(2):
        arrived(codes.at[2 + half], 12 + half)
        arrived(scales.at[2 + half], 16 + half)
        halves[half] = halves[half] + decode(codes_in[2 + half], scales_in[2 + half])
    whole = jnp.concatenate(halves, axis=0)
    outer = lax.dot_general(
        whole, whole, (((0,), (0,)), ((), ())),
        precision=lax.Precision.HIGHEST, preferred_element_type=jnp.float32,
    )
    partial[...] = outer[RANK:]
    send(partial, partner, 6, sibling)
    arrived(partner, 6)
    rounded = (partial[...] + partner[...]).astype(jnp.bfloat16)
    def iota(rows_, lanes, axis):
        return lax.broadcasted_iota(jnp.int32, (rows_, lanes), axis)

    def matrix(condition):
        return jnp.where(condition, 1.0, 0.0).astype(jnp.bfloat16)

    twice = matrix(iota(2 * RANK, 2 * RANK, 0) == lax.rem(iota(2 * RANK, 2 * RANK, 1), RANK))
    doubled = jnp.dot(rounded, twice, preferred_element_type=jnp.float32)
    parity = lax.rem(iota(RANK, 2 * RANK, 0), 2) == lax.div(iota(RANK, 2 * RANK, 1), RANK)
    doubled = jnp.where(parity, doubled, 0.0).astype(jnp.bfloat16)
    to, come = iota(32, RANK, 0), iota(32, RANK, 1)
    order = matrix(
        jnp.logical_and(
            lax.div(to, 8) == lax.rem(lax.div(come, 4), 4),
            lax.rem(to, 8) == lax.div(come, 16) * 2 + lax.div(lax.rem(come, 4), 2),
        )
    )
    ordered = jnp.dot(order, doubled, preferred_element_type=jnp.float32)
    factor[...] = ordered.reshape(4, 8, 2 * RANK)
    for k in PLANE:
        send(factor.at[lax.rem(px + k // 4, 4)], factors.at[plane], 7, beside(k))
    factors[plane] = factor[px]

    arrived(blocks, 5)
    b = blocks[...].astype(jnp.float32)
    gathered[run] = (summed[group].astype(jnp.float32) + b[0] + (b[1] + b[2])).astype(jnp.bfloat16)
    for k in (2, 1, 3):
        send(gathered.at[run], gathered.at[run], 8, along(k))
    arrived(factors.at[pl.ds(0, NEAR - 1)], 7)
    left_side = factors[...].reshape(NEAR * 8, 2 * RANK).astype(jnp.bfloat16)
    which = lax.rem(iota(NEAR * 8, HALF, 0), 8)
    arrived(gathered.at[pl.ds(0, RUNS - 1)], 8)
    scores = jnp.zeros((NEAR * 8, HALF), jnp.float32)
    for k in range(2 * RUNS):
        piece = gathered[k // 2, :, :, (k % 2) * 128 : (k % 2) * 128 + 128]
        right_side = jnp.concatenate([piece[0]] * 4 + [piece[1]] * 4, axis=0)
        term = lax.dot_general(left_side, right_side, contract, preferred_element_type=jnp.float32)
        scores += jnp.where(which == k, term, 0.0)
    mine = lax.div(lax.rem(iota(NEAR * 8, HALF, 1), 64), 16) == py
    scores = jnp.where(mine, scores, 0.0)
    part[...] = jnp.sum(scores.reshape(NEAR, 8, HALF), axis=1, keepdims=True)
    for k in PLANE:
        there = lax.rem(px + k // 4, 4) * 4 + lax.rem(py + k % 4, 4)
        send(part.at[there], parts.at[plane], 9, beside(k))
    parts[plane] = part[plane]

    left(pair, 0)
    left(query.at[0, pl.ds(0, RUNS - 1)], 1)
    left(hess.at[pl.ds(0, 3)], 2)
    left(query.at[pl.ds(0, 3)], 3)
    for slot in range(4):
        left(codes.at[slot], 10 + slot)
        left(scales.at[slot], 14 + slot)
    left(others, 4)
    left(partner, 6)
    left(factors.at[pl.ds(0, NEAR - 1)], 7)
    left(gathered.at[pl.ds(0, RUNS - 1)], 8)
    left(blocks, 5)
    arrived(parts.at[pl.ds(0, NEAR - 1)], 9)
    out[...] = jnp.sum(parts[...], axis=0)
    left(parts.at[pl.ds(0, NEAR - 1)], 9)


def on_device(activations, output_grads, projection, token_counts, hessian_inverse, queries):
    anywhere = pl.BlockSpec(memory_space=pltpu.HBM)
    bf16, f32 = jnp.bfloat16, jnp.float32
    scratch = [
        pltpu.VMEM((1, 256, 1024), bf16),
        pltpu.VMEM((1, 256, 1024), bf16),
        pltpu.VMEM((1024, 128), bf16),
        pltpu.SMEM((1,), jnp.int32),
        pltpu.VMEM((2, HALF, 128), f32),
        pltpu.VMEM((HALF, 128), f32),
        pltpu.VMEM((4, HALF // 2, 128), jnp.int16),
        pltpu.VMEM((4, HALF // 2, 128), jnp.int16),
        pltpu.VMEM((4, 8, 128), f32),
        pltpu.VMEM((4, 8, 128), f32),
        pltpu.VMEM((RANK, 128), f32),
        pltpu.VMEM((RANK, 128), f32),
        pltpu.VMEM((4, 8, 128), f32),
        pltpu.VMEM((NEAR, 8, 128), f32),
        pltpu.VMEM((4, RANK, 512), bf16),
        pltpu.VMEM((4, RUNS, 16, 512), bf16),
        pltpu.VMEM((RUNS, 2, 16, 4 * RANK), f32),
        pltpu.VMEM((RUNS, 2, 16, 4 * RANK), f32),
        pltpu.VMEM((RUNS, 2, 16, 4 * RANK), f32),
        pltpu.VMEM((RUNS, 2, 16, 4 * RANK), bf16),
        pltpu.VMEM((RUNS - 1, 2, 16, 4 * RANK), bf16),
        pltpu.VMEM((RUNS, 2, 16, 4 * RANK), bf16),
        pltpu.VMEM((NEAR, 1, HALF), f32),
        pltpu.VMEM((NEAR, 1, HALF), f32),
        pltpu.SemaphoreType.DMA((6,)),
        pltpu.SemaphoreType.DMA((18,)),
        pltpu.SemaphoreType.DMA((18,)),
        pltpu.SemaphoreType.DMA((RUNS - 1,)),
        pltpu.SemaphoreType.DMA((RUNS,)),
    ]
    return pl.pallas_call(
        attribute,
        out_shape=jax.ShapeDtypeStruct((1, HALF), f32),
        in_specs=[anywhere] * 6,
        out_specs=pl.BlockSpec(memory_space=pltpu.VMEM),
        scratch_shapes=scratch,
        compiler_params=pltpu.CompilerParams(
            collective_id=0, has_side_effects=True, vmem_limit_bytes=60 << 20
        ),
        cost_estimate=pl.CostEstimate(flops=200_000_000, bytes_accessed=1_500_000, transcendentals=0),
        name="attribute",
    )(activations, output_grads, projection, token_counts, hessian_inverse, queries)


def solution(mesh):
    placed = (
        P("dp", None, "tensor"),
        P("dp", None, "tensor"),
        P("tensor", None),
        P("dp"),
        P("dp", "tensor"),
        P("dp", "tensor"),
    )
    return jax.shard_map(
        on_device, mesh=mesh, in_specs=placed, out_specs=P("dp", "tensor"), check_vma=False
    )
```
